512 devices in a mesh: dp: 32 (over x_lo, z), head: 16 (over y, x_hi, core).
Axes of the slice: x: 4 (x_hi: 2, x_lo: 2; x = x_hi * 2 + x_lo), y: 4, z: 16, core: 2. Of those that a mesh axis runs over, the one named last changes fastest.
Arguments:
- q_latent: bfloat16 [24576, 1536], P('dp'), may hold values from -65 to 65
- kv_latent: bfloat16 [24576, 512], P('dp'), may hold values from -65 to 65
- q_cotangent: bfloat16 [24576, 6144], P('dp', 'head'), may hold values from -36 to 36
- kv_cotangent: bfloat16 [24576, 8192], P('dp', 'head'), may hold values from -36 to 36
Outputs:
- q_update: float32 [1536, 6144], P('dp', 'head')
- kv_update: float32 [512, 8192], P('dp', 'head')
The draws below stay inside these ranges and needn't reach their ends.
All inputs are finite; a program needn't handle non-finite values.
Results may differ from the reference program's by a relative error of at most 0.0004.
Values sent between devices are 32-bit elements; how exact they have to be, the bound alone decides.
No kernel may reach another device: no remote copies, remote signals or barrier semaphores. Data moves between devices by JAX's collectives and lax.ppermute only.
A program may use at most 64 MiB of HBM per device.

```python
import math
import jax
import jax.numpy as jnp
from jax import lax

QRANK = 1536
KVRANK = 512
HEADS = 32
QDIM = 192
KVDIM = 256
ITERS = 5
TOKENS = 24576


def combine(base_key, rows, cols):
    normal_part = jax.random.normal(base_key, (rows, cols), jnp.float32)
    mixed = normal_part
    return jnp.clip(mixed, -4.0, 4.0)


def scale_values(scale_key, values, rising, col_lo, col_hi):
    row_key, col_key = jax.random.split(scale_key, 2)
    rows, cols = values.shape
    row_scale = jnp.exp(jax.random.uniform(row_key, (rows, 1), jnp.float32, math.log(0.3), math.log(3.0)))
    col_scale = jnp.exp(jax.random.uniform(col_key, (1, cols), jnp.float32, math.log(col_lo), math.log(col_hi)))
    ramp = jnp.arange(cols, dtype=jnp.float32)[None, :] / cols
    return values * row_scale * col_scale * jnp.exp(rising * math.log(3.0) * ramp)


def draw_q_latent(key, part):
    key = jax.random.fold_in(key, 11)
    base_key = jax.random.fold_in(key, 0)
    scale_key = jax.random.fold_in(key, 2)
    values = combine(base_key, TOKENS, QRANK)
    return scale_values(scale_key, values, 1.0, 0.55, 1.8).astype(jnp.bfloat16)


def draw_kv_latent(key, part):
    key = jax.random.fold_in(key, 23)
    base_key = jax.random.fold_in(key, 0)
    scale_key = jax.random.fold_in(key, 2)
    values = combine(base_key, TOKENS, KVRANK)
    return scale_values(scale_key, values, 1.0, 0.55, 1.8).astype(jnp.bfloat16)


def draw_q_cotangent(key, part):
    key = jax.random.fold_in(key, 37)
    base_key = jax.random.fold_in(key, 0)
    scale_key = jax.random.fold_in(key, 2)
    values = combine(base_key, TOKENS, HEADS * QDIM)
    return scale_values(scale_key, values, 0.0, 0.3, 3.0).astype(jnp.bfloat16)


def draw_kv_cotangent(key, part):
    key = jax.random.fold_in(key, 41)
    base_key = jax.random.fold_in(key, 0)
    scale_key = jax.random.fold_in(key, 2)
    values = combine(base_key, TOKENS, HEADS * KVDIM)
    return scale_values(scale_key, values, 0.0, 0.3, 3.0).astype(jnp.bfloat16)


def setup_inputs(seed: int = 0) -> dict:
    streams_of = jax.random.split(jax.random.key(seed), 5)
    return {
        "q_latent": draw_q_latent(jax.random.fold_in(streams_of[4], 71), 0),
        "kv_latent": draw_kv_latent(jax.random.fold_in(streams_of[4], 71), 0),
        "q_cotangent": draw_q_cotangent(jax.random.fold_in(streams_of[4], 71), 0),
        "kv_cotangent": draw_kv_cotangent(jax.random.fold_in(streams_of[4], 71), 0),
    }


COEF_A = 3.4445
COEF_B = -4.775
COEF_C = 2.0315
EPSILON = 1e-06

def orthogonalize(gradient, width):
    rows_total = gradient.shape[0]
    blocks = gradient.reshape(rows_total, HEADS, width)
    squares = lax.optimization_barrier(jnp.sum(blocks * blocks, axis=(0, 2)))
    current = blocks * lax.rsqrt(squares + EPSILON)[None, :, None]
    for sweep_idx in range(ITERS):
        gram_mat = jnp.einsum('rhi,rhj->hij', current, current, precision=lax.Precision.HIGHEST)
        square_mat = jnp.einsum('hij,hjk->hik', gram_mat, gram_mat, precision=lax.Precision.HIGHEST)
        poly_mat = COEF_B * gram_mat + COEF_C * square_mat
        current = COEF_A * current + jnp.einsum('rhi,hij->rhj', current, poly_mat, precision=lax.Precision.HIGHEST)
    return (current * math.sqrt(rows_total)).reshape(rows_total, HEADS * width)

def reference(q_latent, kv_latent, q_cotangent, kv_cotangent):
    dims = (((0,), (0,)), ((), ()))
    q_grad = lax.dot_general(q_latent, q_cotangent, dims, preferred_element_type=jnp.float32)
    kv_grad = lax.dot_general(kv_latent, kv_cotangent, dims, preferred_element_type=jnp.float32)
    return (orthogonalize(q_grad, QDIM), orthogonalize(kv_grad, KVDIM))
```

```python
import functools
import math

import jax
import jax.numpy as jnp
from jax import lax
from jax.experimental import pallas as pl
from jax.experimental.pallas import tpu as pltpu
from jax.sharding import Mesh, PartitionSpec as P

QRANK = 1536
KVRANK = 512
QDIM = 192
KVDIM = 256
ITERS = 5
RESTART = 3

COEF_A = 3.4445
COEF_B = -4.775
COEF_C = 2.0315
EPSILON = 1e-06

LANES = 256
QTILES = QRANK // 2 // LANES
QPART = QTILES * QDIM
QUARTER = QPART + KVDIM
CUT = QUARTER // 2
GRAMS = QDIM + KVDIM
ZHIGH = 8
QOWN = QRANK // 32
KVOWN = KVRANK // 32
OWN = QOWN + KVOWN

PARAMS = pltpu.CompilerParams(vmem_limit_bytes=48 * 1024 * 1024)
VMEM = pl.BlockSpec(memory_space=pltpu.VMEM)
F32 = jnp.float32


def dot(lhs, rhs, dims):
    return lax.dot_general(
        lhs, rhs, (dims, ((), ())), precision=lax.Precision.HIGHEST, preferred_element_type=F32
    )


def mul(lhs, rhs):
    return dot(lhs, rhs, ((1,), (0,)))


def gradient_kernel(ql, kl, qc, kc, a_send, a_keep, b_send, b_keep):
    x, z = lax.axis_index("x"), lax.axis_index("zl")
    for away_h in (1, 0):
        second = (x ^ away_h) == 1
        qh = jnp.where(second, qc[:, QDIM:], qc[:, :QDIM])
        kh = jnp.where(second, kc[:, KVDIM:], kc[:, :KVDIM])
        a_out = a_send if away_h else a_keep
        for away_p in (1, 0):
            half = z ^ away_p
            b_out = b_send if away_p else b_keep
            for tile in range(QTILES):
                start = pl.multiple_of(half * (QRANK // 2) + tile * LANES, LANES)
                part = lax.dot_general(
                    qh, ql[:, pl.ds(start, LANES)], (((0,), (0,)), ((), ())), preferred_element_type=F32
                )
                low = tile * QDIM
                inside = min(max(CUT - low, 0), QDIM)
                if inside:
                    a_out[away_p, low : low + inside, :] = part[:inside]
                if inside < QDIM:
                    b_out[away_h, low + inside - CUT : low + QDIM - CUT, :] = part[inside:]
            start = pl.multiple_of(half * LANES, LANES)
            part = lax.dot_general(
                kh, kl[:, pl.ds(start, LANES)], (((0,), (0,)), ((), ())), preferred_element_type=F32
            )
            b_out[away_h, QPART - CUT :, :] = part


def put_grams(out, q_tiles, kv):
    q_gram = sum(dot(tile, tile, ((1,), (1,))) for tile in q_tiles)
    out[:QDIM, :QDIM] = q_gram
    out[:QDIM, QDIM:] = jnp.zeros((QDIM, LANES - QDIM), F32)
    out[QDIM:, :] = dot(kv, kv, ((1,), (1,)))


def gram_kernel(y, out):
    put_grams(out, [y[t * QDIM : (t + 1) * QDIM, :] for t in range(QTILES)], y[QPART:, :])


def identity(size):
    rows = lax.broadcasted_iota(jnp.int32, (size, size), 0)
    return rows == lax.broadcasted_iota(jnp.int32, (size, size), 1)


def steps(grams, count):
    products = [None] * len(grams)
    for index in range(count):
        squares = [mul(gram, gram) for gram in grams]
        polys = [COEF_B * gram + COEF_C * square for gram, square in zip(grams, squares)]
        for k, poly in enumerate(polys):
            if products[k] is None:
                products[k] = jnp.where(identity(poly.shape[0]), COEF_A + poly, poly)
            else:
                products[k] = COEF_A * products[k] + mul(products[k], poly)
        if index + 1 < count:
            inner = [COEF_A * gram + mul(gram, poly) for gram, poly in zip(grams, polys)]
            grams = [COEF_A * mid + mul(poly, mid) for mid, poly in zip(inner, polys)]
    return products


def first_kernel(mine, other, y, x_out, out):
    total = mine[...] + other[...]
    q_gram, kv_gram = total[:QDIM, :QDIM], total[QDIM:, :]
    grams, scales = [], []
    for gram in (q_gram, kv_gram):
        trace = jnp.sum(jnp.where(identity(gram.shape[0]), gram, 0.0))
        scale = lax.rsqrt(jnp.full((1, LANES), trace + EPSILON, F32))
        scales.append(scale)
        wide = scale[:, : gram.shape[0]]
        grams.append(gram * wide * wide)
    q_prod, kv_prod = steps(grams, RESTART)
    tiles = []
    for t in range(QTILES):
        rows = slice(t * QDIM, (t + 1) * QDIM)
        tile = mul(q_prod, y[rows, :] * scales[0])
        x_out[rows, :] = tile
        tiles.append(tile)
    kv = mul(kv_prod, y[QPART:, :] * scales[1])
    x_out[QPART:, :] = kv
    put_grams(out, tiles, kv)


def second_kernel(mine, other, xt, out, q_scratch, kv_scratch):
    total = mine[...] + other[...]
    q_prod, kv_prod = steps([total[:QDIM, :QDIM], total[QDIM:, :]], ITERS - RESTART)
    for t in range(QTILES):
        q_scratch[t * LANES : (t + 1) * LANES, :] = dot(xt[t * QDIM : (t + 1) * QDIM, :], q_prod, ((0,), (0,)))
    kv_scratch[...] = dot(xt[QPART:, :], kv_prod, ((0,), (0,)))
    high = lax.axis_index("zh")
    for k in range(2):
        q_start = pl.multiple_of(high * (2 * QOWN) + k * QOWN, 8)
        kv_start = pl.multiple_of(high * (2 * KVOWN) + k * KVOWN, 8)
        q_rows = q_scratch[pl.ds(q_start, QOWN), :] * math.sqrt(QRANK)
        kv_rows = kv_scratch[pl.ds(kv_start, KVOWN), :] * math.sqrt(KVRANK)
        for owner in range(2):
            out[2 * owner + k, :QOWN, :QDIM] = q_rows
            out[2 * owner + k, :QOWN, QDIM:] = jnp.zeros((QOWN, LANES - QDIM), F32)
            out[2 * owner + k, QOWN:, :] = kv_rows


def join_kernel(got, q_out, kv_out):
    x = lax.axis_index("x")
    for head in range(2):
        block = got[2 * head + x]
        q_out[:, head * QDIM : (head + 1) * QDIM] = block[:QOWN, :QDIM]
        kv_out[:, head * KVDIM : (head + 1) * KVDIM] = block[QOWN:, :]


def shape(*dims):
    return jax.ShapeDtypeStruct(dims, F32)


def call(kernel, outs, inputs, scratch=()):
    single = not isinstance(outs, tuple)
    return pl.pallas_call(
        kernel,
        out_shape=outs,
        in_specs=[VMEM] * inputs,
        out_specs=VMEM if single else (VMEM,) * len(outs),
        scratch_shapes=list(scratch),
        compiler_params=PARAMS,
    )


PAIR = [(0, 1), (1, 0)]


def body(q_latent, kv_latent, q_cotangent, kv_cotangent):
    half = shape(2, CUT, LANES)
    a_send, a_keep, b_send, b_keep = call(gradient_kernel, (half,) * 4, 4)(
        q_latent, kv_latent, q_cotangent, kv_cotangent
    )
    a_got = lax.ppermute(a_send, "x", PAIR)
    b_got = lax.ppermute(b_send, "zl", PAIR)
    a_next = lax.ppermute(a_keep[1] + a_got[1], "zl", PAIR)
    b_next = lax.ppermute(b_keep[1] + b_got[1], "x", PAIR)
    quarter = jnp.concatenate((a_keep[0] + a_got[0] + a_next, b_keep[0] + b_got[0] + b_next), axis=0)
    spread = lax.all_to_all(quarter.reshape(ZHIGH, QUARTER // ZHIGH, LANES), "zh", 0, 0)
    y = lax.all_gather(jnp.sum(spread, axis=0), "zh", axis=0, tiled=True)
    grams = shape(GRAMS, LANES)
    mine = call(gram_kernel, grams, 1)(y)
    other = lax.ppermute(mine, "zl", PAIR)
    xt, mine = call(first_kernel, (shape(QUARTER, LANES), grams), 3)(mine, other, y)
    other = lax.ppermute(mine, "zl", PAIR)
    ready = call(
        second_kernel,
        shape(4, OWN, LANES),
        3,
        (pltpu.VMEM((QRANK // 2, QDIM), F32), pltpu.VMEM((KVRANK // 2, KVDIM), F32)),
    )(mine, other, xt)
    got = lax.all_to_all(ready, ("x", "zl"), 0, 0)
    return call(join_kernel, (shape(QOWN, 2 * QDIM), shape(KVOWN, 2 * KVDIM)), 1)(got)


def solution(mesh):
    fine = Mesh(mesh.devices.reshape(2, ZHIGH, 2, -1), ("x", "zh", "zl", "head"))
    rows = ("x", "zh", "zl")
    return jax.shard_map(
        body,
        mesh=fine,
        in_specs=(P(rows, None), P(rows, None), P(rows, "head"), P(rows, "head")),
        out_specs=(P(rows, "head"), P(rows, "head")),
        check_vma=False,
    )
```

```python
import math

import jax
import jax.numpy as jnp
from jax import lax
from jax.experimental import pallas as pl
from jax.experimental.pallas import tpu as pltpu
from jax.sharding import Mesh, PartitionSpec as P

QRANK = 1536
KVRANK = 512
QDIM = 192
KVDIM = 256
ITERS = 5
RESTART = 3

COEF_A = 3.4445
COEF_B = -4.775
COEF_C = 2.0315
EPSILON = 1e-06

LANES = 256
QTILES = QRANK // 2 // LANES
QPART = QTILES * QDIM
QUARTER = QPART + KVDIM
CUT = QUARTER // 2
ZHIGH = 8
USED = QUARTER // ZHIGH
SHARD = USED + 7
QOWN = QRANK // 32
KVOWN = KVRANK // 32

MEBI = 1024 * 1024
VMEM = pl.BlockSpec(memory_space=pltpu.VMEM)
F32 = jnp.float32


def dot(lhs, rhs, dims):
    return lax.dot_general(
        lhs, rhs, (dims, ((), ())), precision=lax.Precision.HIGHEST, preferred_element_type=F32
    )


def mul(lhs, rhs):
    return dot(lhs, rhs, ((1,), (0,)))


def products(cot, start, stop, lat):
    return lax.dot_general(
        cot[:, start:stop], lat, (((0,), (0,)), ((), ())), preferred_element_type=F32
    )


def fill(q_cot, kv_cot, q_lat, kv_lat, a_out, b_out):
    for tile in range(QTILES):
        lat = q_lat(tile)
        low = tile * QDIM
        inside = min(max(CUT - low, 0), QDIM)
        if inside and a_out is not None:
            a_out[low : low + inside, :] = products(q_cot, 0, inside, lat)
        if inside < QDIM and b_out is not None:
            b_out[low + inside - CUT : low + QDIM - CUT, :] = products(q_cot, inside, QDIM, lat)
    if b_out is not None:
        b_out[QPART - CUT :, :] = products(kv_cot, 0, KVDIM, kv_lat)


def heads(qc, kc, x, away):
    second = (x ^ away) == 1
    q_cot = jnp.where(second, qc[:, QDIM:], qc[:, :QDIM])
    return q_cot, jnp.where(second, kc[:, KVDIM:], kc[:, :KVDIM])


def send_kernel(ql, kl, qc, kc, a_send, b_send, qc_v, kc_v, ql_v, kl_v, sems):
    x, z = lax.axis_index("x"), lax.axis_index("zl")
    q_half, kv_half = QRANK // 2, KVRANK // 2
    copies = [pltpu.make_async_copy(qc, qc_v, sems.at[0])]
    for away in (1, 0):
        lanes = pl.ds(pl.multiple_of((z ^ away) * q_half, LANES), q_half)
        copies.append(pltpu.make_async_copy(ql.at[:, lanes], ql_v.at[away], sems.at[2 - away]))
    lanes = pl.ds(pl.multiple_of((z ^ 1) * kv_half, LANES), kv_half)
    copies.append(pltpu.make_async_copy(kc, kc_v, sems.at[3]))
    copies.append(pltpu.make_async_copy(kl.at[:, lanes], kl_v, sems.at[4]))
    for copy in copies:
        copy.start()

    def q_lat(away):
        return lambda tile: ql_v[away, :, tile * LANES : (tile + 1) * LANES]

    copies[0].wait()
    copies[1].wait()
    q_cot = jnp.where((x ^ 1) == 1, qc_v[:, QDIM:], qc_v[:, :QDIM])
    fill(q_cot, None, q_lat(1), None, a_send.at[1], None)
    copies[2].wait()
    fill(q_cot, None, q_lat(0), None, a_send.at[0], None)
    copies[3].wait()
    copies[4].wait()
    for away in (1, 0):
        q_cot, kv_cot = heads(qc_v, kc_v, x, away)
        fill(q_cot, kv_cot, q_lat(1), kl_v[...], None, b_send.at[away])


def keep_kernel(ql, kl, qc, kc, a_keep, b_keep, qc_v, kc_v, ql_v, kl_v, sems):
    x, z = lax.axis_index("x"), lax.axis_index("zl")
    q_half, kv_half = QRANK // 2, KVRANK // 2
    lanes = pl.ds(pl.multiple_of(z * kv_half, LANES), kv_half)
    copies = [
        pltpu.make_async_copy(qc, qc_v, sems.at[0]),
        pltpu.make_async_copy(kc, kc_v, sems.at[1]),
        pltpu.make_async_copy(kl.at[:, lanes], kl_v, sems.at[2]),
    ]
    for away in (0, 1):
        lanes = pl.ds(pl.multiple_of((z ^ away) * q_half, LANES), q_half)
        copies.append(pltpu.make_async_copy(ql.at[:, lanes], ql_v.at[away], sems.at[3 + away]))
    for copy in copies:
        copy.start()
    for copy in copies:
        copy.wait()

    def q_lat(away):
        return lambda tile: ql_v[away, :, tile * LANES : (tile + 1) * LANES]

    q_cot, kv_cot = heads(qc_v, kc_v, x, 1)
    fill(q_cot, kv_cot, q_lat(0), kl_v[...], None, b_keep.at[1])
    q_cot, kv_cot = heads(qc_v, kc_v, x, 0)
    fill(q_cot, kv_cot, q_lat(1), None, a_keep.at[1], None)
    fill(q_cot, kv_cot, q_lat(0), kl_v[...], a_keep.at[0], b_keep.at[0])


def place_kernel(a_keep, a_got, a_next, b_keep, b_got, b_next, out):
    for index in range(ZHIGH):
        for keep, got, last, low in ((a_keep, a_got, a_next, 0), (b_keep, b_got, b_next, CUT)):
            start, stop = max(index * USED, low), min((index + 1) * USED, low + CUT)
            if start < stop:
                rows = slice(start - low, stop - low)
                where = index * SHARD + start - index * USED
                out[where : where + stop - start, :] = keep[0, rows, :] + got[0, rows, :] + last[rows, :]
        out[index * SHARD + USED : (index + 1) * SHARD, :] = jnp.zeros((SHARD - USED, LANES), F32)


def identity(size):
    rows = lax.broadcasted_iota(jnp.int32, (size, size), 0)
    return rows == lax.broadcasted_iota(jnp.int32, (size, size), 1)


def steps(gram, count):
    product = None
    for index in range(count):
        poly = COEF_B * gram + COEF_C * mul(gram, gram)
        if product is None:
            product = jnp.where(identity(poly.shape[0]), COEF_A + poly, poly)
        else:
            product = COEF_A * product + mul(product, poly)
        if index + 1 < count:
            inner = COEF_A * gram + mul(gram, poly)
            gram = COEF_A * inner + mul(poly, inner)
    return product


def orthogonalize(tiles, norm, rows):
    gram = sum(dot(tile, tile, ((1,), (1,))) for tile in tiles)
    size = gram.shape[0]
    trace = jnp.sum(jnp.where(identity(size), gram, 0.0))
    scale = lax.rsqrt(jnp.full((1, LANES), trace + EPSILON, F32))
    wide = scale[:, :size]
    product = steps(gram * wide * wide, RESTART)
    tiles = [mul(product, tile * scale) for tile in tiles]
    gram = sum(dot(tile, tile, ((1,), (1,))) for tile in tiles)
    product = steps(gram, ITERS - RESTART)
    for index, tile in enumerate(tiles):
        rows[index * LANES : (index + 1) * LANES, :] = dot(tile, product, ((0,), (0,))) * norm


def update_kernel(y, q_other, kv_other, out, q_rows, kv_rows):
    z, high = lax.axis_index("zl"), lax.axis_index("zh")

    def q_tiles(ref):
        return [ref[t * QDIM : (t + 1) * QDIM, :] for t in range(QTILES)]

    @pl.when(z == 0)
    def _():
        orthogonalize(q_tiles(y) + q_tiles(q_other), math.sqrt(QRANK), q_rows)
        for half in range(2):
            for k in range(2):
                start = pl.multiple_of(half * (QRANK // 2) + (2 * high + k) * QOWN, 8)
                out[2 * half + k, :, :QDIM] = q_rows[pl.ds(start, QOWN), :]
                out[2 * half + k, :, QDIM:] = jnp.zeros((QOWN, LANES - QDIM), F32)

    @pl.when(z == 1)
    def _():
        orthogonalize([kv_other[...], y[QPART:, :]], math.sqrt(KVRANK), kv_rows)
        for half in range(2):
            for k in range(2):
                start = pl.multiple_of(half * (KVRANK // 2) + (2 * high + k) * KVOWN, 8)
                out[2 * half + k, :KVOWN, :] = kv_rows[pl.ds(start, KVOWN), :]
                out[2 * half + k, KVOWN:, :] = jnp.zeros((QOWN - KVOWN, LANES), F32)


def join_kernel(got, q_out, kv_out):
    for head in range(2):
        q_out[:, head * QDIM : (head + 1) * QDIM] = got[2 * head, :, :QDIM]
        kv_out[:, head * KVDIM : (head + 1) * KVDIM] = got[2 * head + 1, :KVOWN, :]


def shape(*dims):
    return jax.ShapeDtypeStruct(dims, F32)


def call(kernel, outs, inputs, scratch=(), space=pltpu.VMEM, cost=None, vmem=24):
    single = not isinstance(outs, tuple)
    return pl.pallas_call(
        kernel,
        out_shape=outs,
        in_specs=[pl.BlockSpec(memory_space=space)] * inputs,
        out_specs=VMEM if single else (VMEM,) * len(outs),
        scratch_shapes=list(scratch),
        compiler_params=pltpu.CompilerParams(vmem_limit_bytes=vmem * MEBI),
        cost_estimate=cost,
    )


PAIR = [(0, 1), (1, 0)]


def body(q_latent, kv_latent, q_cotangent, kv_cotangent):
    half = shape(2, CUT, LANES)
    tokens = q_latent.shape[0]
    scratch = [
        pltpu.VMEM(dims, q_latent.dtype)
        for dims in (q_cotangent.shape, kv_cotangent.shape, (2, tokens, QRANK // 2), (tokens, KVRANK // 2))
    ]
    scratch.append(pltpu.SemaphoreType.DMA((5,)))
    args = (q_latent, kv_latent, q_cotangent, kv_cotangent)
    cost = pl.CostEstimate(flops=2 * tokens * 2 * 2 * CUT * LANES, bytes_accessed=8 << 20, transcendentals=0)
    a_send, b_send = call(send_kernel, (half, half), 4, scratch, pltpu.HBM, cost, 60)(*args)
    a_got = lax.ppermute(a_send, "x", PAIR)
    b_got = lax.ppermute(b_send, "zl", PAIR)
    a_keep, b_keep = call(keep_kernel, (half, half), 4, scratch, pltpu.HBM, cost, 60)(*args)
    a_next = lax.ppermute(a_keep[1] + a_got[1], "zl", PAIR)
    b_next = lax.ppermute(b_keep[1] + b_got[1], "x", PAIR)
    placed = call(place_kernel, shape(ZHIGH * SHARD, LANES), 6)(a_keep, a_got, a_next, b_keep, b_got, b_next)
    part = lax.optimization_barrier(lax.psum_scatter(placed, "zh", scatter_dimension=0, tiled=True))
    y = lax.all_gather(part[:USED], "zh", axis=0, tiled=True)
    q_other = lax.ppermute(y[:QPART], "zl", [(1, 0)])
    kv_other = lax.ppermute(y[QPART:], "zl", [(0, 1)])
    rows = (pltpu.VMEM((QRANK, QDIM), F32), pltpu.VMEM((KVRANK, KVDIM), F32))
    ready = call(update_kernel, shape(4, QOWN, LANES), 3, rows)(y, q_other, kv_other)
    got = lax.all_to_all(ready, ("x", "zl"), 0, 0)
    return call(join_kernel, (shape(QOWN, 2 * QDIM), shape(KVOWN, 2 * KVDIM)), 1)(got)


def solution(mesh):
    fine = Mesh(mesh.devices.reshape(2, ZHIGH, 2, -1), ("x", "zh", "zl", "head"))
    rows = ("x", "zh", "zl")
    return jax.shard_map(
        body,
        mesh=fine,
        in_specs=(P(rows, None), P(rows, None), P(rows, "head"), P(rows, "head")),
        out_specs=(P(rows, "head"), P(rows, "head")),
        check_vma=False,
    )
```

```python
import math

import jax
import jax.numpy as jnp
from jax import lax
from jax.experimental import pallas as pl
from jax.experimental.pallas import tpu as pltpu
from jax.sharding import Mesh, PartitionSpec as P

QRANK = 1536
KVRANK = 512
QDIM = 192
KVDIM = 256
ITERS = 5
RESTART = 3

COEF_A = 3.4445
COEF_B = -4.775
COEF_C = 2.0315
EPSILON = 1e-06

LANES = 256
QTILES = QRANK // LANES
KVTILES = KVRANK // LANES
HEAD_ROWS = QTILES * QDIM + KVTILES * KVDIM
PART = HEAD_ROWS // 2
CUT = PART // 2
QHERE = PART // QDIM
QREST = PART - QHERE * QDIM
QMORE = QTILES * QDIM - PART
ZHIGH = 8
USED = PART // ZHIGH
SHARD = USED + 7
QOWN = QRANK // 32
KVOWN = KVRANK // 32
MEBI = 1024 * 1024
VMEM = pl.BlockSpec(memory_space=pltpu.VMEM)
F32 = jnp.float32


def dot(lhs, rhs, dims):
    return lax.dot_general(
        lhs, rhs, (dims, ((), ())), precision=lax.Precision.HIGHEST, preferred_element_type=F32
    )


def mul(lhs, rhs):
    return dot(lhs, rhs, ((1,), (0,)))


def products(cot, start, stop, lat):
    return lax.dot_general(
        cot[:, start:stop], lat, (((0,), (0,)), ((), ())), preferred_element_type=F32
    )


def fill(part, low, high, q_cot, kv_cot, ql, kl, out):
    base = part * PART
    at = base + low
    while at < base + high:
        in_q = at < QTILES * QDIM
        width, first, cot, lat = (QDIM, 0, q_cot, ql) if in_q else (KVDIM, QTILES * QDIM, kv_cot, kl)
        tile, start = divmod(at - first, width)
        stop = min(width, start + base + high - at)
        block = products(cot, start, stop, lat[:, tile * LANES : (tile + 1) * LANES])
        out[at - base - low : at - base - low + stop - start, :] = block
        at += stop - start


def heads(qc, kc, x, away):
    second = (x ^ away) == 1
    q_cot = jnp.where(second, qc[:, QDIM:], qc[:, :QDIM])
    return q_cot, jnp.where(second, kc[:, KVDIM:], kc[:, :KVDIM])


def send_kernel(ql, kl, qc, kc, a_send, b_send, ql_v, kl_v, qc_v, kc_v, sems):
    x, z = lax.axis_index("x"), lax.axis_index("zl")
    pairs = ((qc, qc_v), (kc, kc_v), (ql, ql_v), (kl, kl_v))
    copies = [pltpu.make_async_copy(src, dst, sems.at[k]) for k, (src, dst) in enumerate(pairs)]
    for copy in copies:
        copy.start()
    for copy in copies:
        copy.wait()
    q_cot, kv_cot = heads(qc_v, kc_v, x, 1)
    for part in range(2):
        fill(part, 0, CUT, q_cot, kv_cot, ql_v, kl_v, a_send.at[z ^ part])
    for part in range(2):

        @pl.when(z != part)
        def _(part=part):
            for away in range(2):
                q_cot, kv_cot = heads(qc_v, kc_v, x, away)
                fill(part, CUT, PART, q_cot, kv_cot, ql_v, kl_v, b_send.at[away])


def keep_kernel(ql, kl, qc, kc, a_keep, b_keep, ql_v, kl_v, qc_v, kc_v, sems):
    x, z = lax.axis_index("x"), lax.axis_index("zl")
    pairs = ((qc, qc_v), (kc, kc_v), (ql, ql_v), (kl, kl_v))
    copies = [pltpu.make_async_copy(src, dst, sems.at[k]) for k, (src, dst) in enumerate(pairs)]
    for copy in copies:
        copy.start()
    for copy in copies:
        copy.wait()
    q_cot, kv_cot = heads(qc_v, kc_v, x, 0)
    for part in range(2):
        fill(part, 0, CUT, q_cot, kv_cot, ql_v, kl_v, a_keep.at[z ^ part])
    for part in range(2):

        @pl.when(z == part)
        def _(part=part):
            for away in range(2):
                q_cot, kv_cot = heads(qc_v, kc_v, x, away)
                fill(part, CUT, PART, q_cot, kv_cot, ql_v, kl_v, b_keep.at[away])


def place_kernel(a_keep, a_got, a_next, b_keep, b_got, b_next, out):
    for index in range(ZHIGH):
        for keep, got, last, low in ((a_keep, a_got, a_next, 0), (b_keep, b_got, b_next, CUT)):
            start, stop = max(index * USED, low), min((index + 1) * USED, low + CUT)
            if start < stop:
                rows = slice(start - low, stop - low)
                where = index * SHARD + start - index * USED
                out[where : where + stop - start, :] = keep[0, rows, :] + got[0, rows, :] + last[rows, :]
        out[index * SHARD + USED : (index + 1) * SHARD, :] = jnp.zeros((SHARD - USED, LANES), F32)


def identity(size):
    rows = lax.broadcasted_iota(jnp.int32, (size, size), 0)
    return rows == lax.broadcasted_iota(jnp.int32, (size, size), 1)


def steps(gram, count):
    product = None
    for index in range(count):
        poly = COEF_B * gram + COEF_C * mul(gram, gram)
        if product is None:
            product = jnp.where(identity(poly.shape[0]), COEF_A + poly, poly)
        else:
            product = COEF_A * product + mul(product, poly)
        if index + 1 < count:
            inner = COEF_A * gram + mul(gram, poly)
            gram = COEF_A * inner + mul(poly, inner)
    return product


def gram_of(wide):
    def term(lhs, rhs):
        return lax.dot_general(lhs, rhs, (((1,), (1,)), ((), ())), preferred_element_type=F32)

    high = wide.astype(jnp.bfloat16)
    rest = wide - high.astype(F32)
    mid = rest.astype(jnp.bfloat16)
    low = (rest - mid.astype(F32)).astype(jnp.bfloat16)
    cross = term(high, mid) + (term(high, low) + 0.5 * term(mid, mid))
    return term(high, high) + (cross + cross.T)


def orthogonalize(tiles, norm, rows):
    wide = jnp.concatenate(tiles, axis=1)
    gram = gram_of(wide)
    trace = jnp.sum(jnp.where(identity(gram.shape[0]), gram, 0.0))
    scale = lax.rsqrt(jnp.full((1, 1), trace + EPSILON, F32))
    product = steps(gram * scale * scale, RESTART)
    wide = mul(product * scale, wide)
    product = steps(gram_of(wide), ITERS - RESTART)
    rows[...] = dot(wide, product * norm, ((0,), (0,)))


def update_kernel(y, other, out, q_rows, kv_rows):
    z, high = lax.axis_index("zl"), lax.axis_index("zh")

    @pl.when(z == 0)
    def _():
        tiles = [y[t * QDIM : (t + 1) * QDIM, :] for t in range(QHERE)]
        tiles.append(jnp.concatenate((y[QHERE * QDIM :, :], other[: QDIM - QREST, :]), axis=0))
        tiles += [other[t * QDIM - PART : (t + 1) * QDIM - PART, :] for t in range(QHERE + 1, QTILES)]
        orthogonalize(tiles, math.sqrt(QRANK), q_rows)
        for half in range(2):
            for k in range(2):
                start = pl.multiple_of(half * (QRANK // 2) + (2 * high + k) * QOWN, 8)
                out[2 * half + k, :, :QDIM] = q_rows[pl.ds(start, QOWN), :]
                out[2 * half + k, :, QDIM:] = jnp.zeros((QOWN, LANES - QDIM), F32)

    @pl.when(z == 1)
    def _():
        tiles = [y[QMORE + t * KVDIM : QMORE + (t + 1) * KVDIM, :] for t in range(KVTILES)]
        orthogonalize(tiles, math.sqrt(KVRANK), kv_rows)
        for half in range(2):
            for k in range(2):
                start = pl.multiple_of(half * (KVRANK // 2) + (2 * high + k) * KVOWN, 8)
                out[2 * half + k, :KVOWN, :] = kv_rows[pl.ds(start, KVOWN), :]
                out[2 * half + k, KVOWN:, :] = jnp.zeros((QOWN - KVOWN, LANES), F32)


def join_kernel(got, q_out, kv_out):
    for head in range(2):
        q_out[:, head * QDIM : (head + 1) * QDIM] = got[2 * head, :, :QDIM]
        kv_out[:, head * KVDIM : (head + 1) * KVDIM] = got[2 * head + 1, :KVOWN, :]


def shape(*dims):
    return jax.ShapeDtypeStruct(dims, F32)


def call(kernel, outs, inputs, scratch=(), space=pltpu.VMEM, cost=None, vmem=24):
    single = not isinstance(outs, tuple)
    return pl.pallas_call(
        kernel,
        out_shape=outs,
        in_specs=[pl.BlockSpec(memory_space=space)] * inputs,
        out_specs=VMEM if single else (VMEM,) * len(outs),
        scratch_shapes=list(scratch),
        compiler_params=pltpu.CompilerParams(vmem_limit_bytes=vmem * MEBI),
        cost_estimate=cost,
    )


PAIR = [(0, 1), (1, 0)]


def body(q_latent, kv_latent, q_cotangent, kv_cotangent):
    half = shape(2, CUT, LANES)
    tokens = q_latent.shape[0]
    args = (q_latent, kv_latent, q_cotangent, kv_cotangent)
    scratch = [pltpu.VMEM(arg.shape, arg.dtype) for arg in args] + [pltpu.SemaphoreType.DMA((4,))]
    cost = pl.CostEstimate(flops=2 * tokens * 2 * 2 * CUT * LANES, bytes_accessed=8 << 20, transcendentals=0)
    a_send, b_send = call(send_kernel, (half, half), 4, scratch, pltpu.HBM, cost, 60)(*args)
    a_got = lax.ppermute(a_send, "x", PAIR)
    b_got = lax.ppermute(b_send, "zl", PAIR)
    a_keep, b_keep = call(keep_kernel, (half, half), 4, scratch, pltpu.HBM, cost, 24)(*args)
    a_next = lax.ppermute(a_keep[1] + a_got[1], "zl", PAIR)
    b_next = lax.ppermute(b_keep[1] + b_got[1], "x", PAIR)
    placed = call(place_kernel, shape(ZHIGH * SHARD, LANES), 6)(a_keep, a_got, a_next, b_keep, b_got, b_next)
    part = lax.optimization_barrier(lax.psum_scatter(placed, "zh", scatter_dimension=0, tiled=True))
    y = lax.all_gather(part[:USED], "zh", axis=0, tiled=True)
    other = lax.ppermute(y[:QMORE], "zl", [(1, 0)])
    rows = (pltpu.VMEM((QRANK, QDIM), F32), pltpu.VMEM((KVRANK, KVDIM), F32))
    ready = call(update_kernel, shape(4, QOWN, LANES), 2, rows)(y, other)
    got = lax.all_to_all(ready, ("x", "zl"), 0, 0)
    return call(join_kernel, (shape(QOWN, 2 * QDIM), shape(KVOWN, 2 * KVDIM)), 1)(got)


def solution(mesh):
    fine = Mesh(mesh.devices.reshape(2, ZHIGH, 2, -1), ("x", "zh", "zl", "head"))
    rows = ("x", "zh", "zl")
    return jax.shard_map(
        body,
        mesh=fine,
        in_specs=(P(rows, None), P(rows, None), P(rows, "head"), P(rows, "head")),
        out_specs=(P(rows, "head"), P(rows, "head")),
        check_vma=False,
    )
```

```python
import math

import jax
import jax.numpy as jnp
from jax import lax
from jax.experimental import pallas as pl
from jax.experimental.pallas import tpu as pltpu
from jax.sharding import Mesh, PartitionSpec as P

QRANK = 1536
KVRANK = 512
QDIM = 192
KVDIM = 256
ITERS = 5
RESTART = 3

COEF_A = 3.4445
COEF_B = -4.775
COEF_C = 2.0315
EPSILON = 1e-06

LANES = 256
QTILES = QRANK // LANES
KVTILES = KVRANK // LANES
HEAD_ROWS = QTILES * QDIM + KVTILES * KVDIM
PART = HEAD_ROWS // 2
CUT = PART // 2
QHERE = PART // QDIM
QREST = PART - QHERE * QDIM
QMORE = QTILES * QDIM - PART
PIECE = 8
PIECES = PART // PIECE
QOWN = QRANK // 32
KVOWN = KVRANK // 32
MEBI = 1024 * 1024
VMEM = pl.BlockSpec(memory_space=pltpu.VMEM)
F32 = jnp.float32


def dot(lhs, rhs, dims):
    return lax.dot_general(
        lhs, rhs, (dims, ((), ())), precision=lax.Precision.HIGHEST, preferred_element_type=F32
    )


def mul(lhs, rhs):
    return dot(lhs, rhs, ((1,), (0,)))


def products(cot, start, stop, lat):
    return lax.dot_general(
        cot[:, start:stop], lat, (((0,), (0,)), ((), ())), preferred_element_type=F32
    )


def fill(part, low, high, q_cot, kv_cot, ql, kl, out):
    base = part * PART
    at = base + low
    while at < base + high:
        in_q = at < QTILES * QDIM
        width, first, cot, lat = (QDIM, 0, q_cot, ql) if in_q else (KVDIM, QTILES * QDIM, kv_cot, kl)
        tile, start = divmod(at - first, width)
        stop = min(width, start + base + high - at)
        block = products(cot, start, stop, lat[:, tile * LANES : (tile + 1) * LANES])
        out[at - base - low : at - base - low + stop - start, :] = block
        at += stop - start


def heads(qc, kc, x, away):
    second = (x ^ away) == 1
    q_cot = jnp.where(second, qc[:, QDIM:], qc[:, :QDIM])
    return q_cot, jnp.where(second, kc[:, KVDIM:], kc[:, :KVDIM])


def send_kernel(ql, kl, qc, kc, a_send, b_send, ql_v, kl_v, qc_v, kc_v, sems):
    x, z = lax.axis_index("x"), lax.axis_index("zl")
    pairs = ((qc, qc_v), (kc, kc_v), (ql, ql_v), (kl, kl_v))
    copies = [pltpu.make_async_copy(src, dst, sems.at[k]) for k, (src, dst) in enumerate(pairs)]
    for copy in copies:
        copy.start()
    for copy in copies:
        copy.wait()
    q_cot, kv_cot = heads(qc_v, kc_v, x, 1)
    for part in range(2):
        fill(part, 0, CUT, q_cot, kv_cot, ql_v, kl_v, a_send.at[z ^ part])
    for part in range(2):

        @pl.when(z != part)
        def _(part=part):
            for away in range(2):
                q_cot, kv_cot = heads(qc_v, kc_v, x, away)
                fill(part, CUT, PART, q_cot, kv_cot, ql_v, kl_v, b_send.at[away])


def keep_kernel(ql, kl, qc, kc, a_keep, b_keep, ql_v, kl_v, qc_v, kc_v, sems):
    x, z = lax.axis_index("x"), lax.axis_index("zl")
    pairs = ((qc, qc_v), (kc, kc_v), (ql, ql_v), (kl, kl_v))
    copies = [pltpu.make_async_copy(src, dst, sems.at[k]) for k, (src, dst) in enumerate(pairs)]
    for copy in copies:
        copy.start()
    for copy in copies:
        copy.wait()
    q_cot, kv_cot = heads(qc_v, kc_v, x, 0)
    for part in range(2):
        fill(part, 0, CUT, q_cot, kv_cot, ql_v, kl_v, a_keep.at[z ^ part])
    for part in range(2):

        @pl.when(z == part)
        def _(part=part):
            for away in range(2):
                q_cot, kv_cot = heads(qc_v, kc_v, x, away)
                fill(part, CUT, PART, q_cot, kv_cot, ql_v, kl_v, b_keep.at[away])


def add_kernel(a_keep, a_got, a_next, b_keep, b_got, b_next, *outs):
    for k, out in enumerate(outs):
        low = k * PIECE
        keep, got, last = (a_keep, a_got, a_next) if low < CUT else (b_keep, b_got, b_next)
        rows = slice(low % CUT, low % CUT + PIECE)
        out[...] = keep[0, rows, :] + got[0, rows, :] + last[rows, :]


def identity(size):
    rows = lax.broadcasted_iota(jnp.int32, (size, size), 0)
    return rows == lax.broadcasted_iota(jnp.int32, (size, size), 1)


def steps(gram, count):
    product = None
    for index in range(count):
        poly = COEF_B * gram + COEF_C * mul(gram, gram)
        if product is None:
            product = jnp.where(identity(poly.shape[0]), COEF_A + poly, poly)
        else:
            product = COEF_A * product + mul(product, poly)
        if index + 1 < count:
            inner = COEF_A * gram + mul(gram, poly)
            gram = COEF_A * inner + mul(poly, inner)
    return product


def gram_of(wide):
    def term(lhs, rhs):
        return lax.dot_general(lhs, rhs, (((1,), (1,)), ((), ())), preferred_element_type=F32)

    high = wide.astype(jnp.bfloat16)
    rest = wide - high.astype(F32)
    mid = rest.astype(jnp.bfloat16)
    low = (rest - mid.astype(F32)).astype(jnp.bfloat16)
    cross = term(high, mid) + (term(high, low) + 0.5 * term(mid, mid))
    return term(high, high) + (cross + cross.T)


def orthogonalize(tiles, norm, rows):
    wide = jnp.concatenate(tiles, axis=1)
    gram = gram_of(wide)
    trace = jnp.sum(jnp.where(identity(gram.shape[0]), gram, 0.0))
    scale = lax.rsqrt(jnp.full((1, 1), trace + EPSILON, F32))
    product = steps(gram * scale * scale, RESTART)
    wide = mul(product * scale, wide)
    product = steps(gram_of(wide), ITERS - RESTART)
    rows[...] = dot(wide, product * norm, ((0,), (0,)))


def update_kernel(*refs):
    pieces, (other, out, q_rows, kv_rows) = refs[:PIECES], refs[PIECES:]

    def y(low, high):
        return jnp.concatenate([ref[...] for ref in pieces[low // PIECE : high // PIECE]], axis=0)

    z, high = lax.axis_index("zl"), lax.axis_index("zh")

    @pl.when(z == 0)
    def _():
        tiles = [y(t * QDIM, (t + 1) * QDIM) for t in range(QHERE)]
        tiles.append(jnp.concatenate((y(QHERE * QDIM, PART), other[: QDIM - QREST, :]), axis=0))
        tiles += [other[t * QDIM - PART : (t + 1) * QDIM - PART, :] for t in range(QHERE + 1, QTILES)]
        orthogonalize(tiles, math.sqrt(QRANK), q_rows)
        for half in range(2):
            for k in range(2):
                start = pl.multiple_of(half * (QRANK // 2) + (2 * high + k) * QOWN, 8)
                out[2 * half + k, :, :QDIM] = q_rows[pl.ds(start, QOWN), :]
                out[2 * half + k, :, QDIM:] = jnp.zeros((QOWN, LANES - QDIM), F32)

    @pl.when(z == 1)
    def _():
        tiles = [y(QMORE + t * KVDIM, QMORE + (t + 1) * KVDIM) for t in range(KVTILES)]
        orthogonalize(tiles, math.sqrt(KVRANK), kv_rows)
        for half in range(2):
            for k in range(2):
                start = pl.multiple_of(half * (KVRANK // 2) + (2 * high + k) * KVOWN, 8)
                out[2 * half + k, :KVOWN, :] = kv_rows[pl.ds(start, KVOWN), :]
                out[2 * half + k, KVOWN:, :] = jnp.zeros((QOWN - KVOWN, LANES), F32)


def join_kernel(got, q_out, kv_out):
    for head in range(2):
        q_out[:, head * QDIM : (head + 1) * QDIM] = got[2 * head, :, :QDIM]
        kv_out[:, head * KVDIM : (head + 1) * KVDIM] = got[2 * head + 1, :KVOWN, :]


def shape(*dims):
    return jax.ShapeDtypeStruct(dims, F32)


def call(kernel, outs, inputs, scratch=(), space=pltpu.VMEM, cost=None, vmem=24):
    single = not isinstance(outs, tuple)
    return pl.pallas_call(
        kernel,
        out_shape=outs,
        in_specs=[pl.BlockSpec(memory_space=space)] * inputs,
        out_specs=VMEM if single else (VMEM,) * len(outs),
        scratch_shapes=list(scratch),
        compiler_params=pltpu.CompilerParams(vmem_limit_bytes=vmem * MEBI),
        cost_estimate=cost,
    )


PAIR = [(0, 1), (1, 0)]


def body(q_latent, kv_latent, q_cotangent, kv_cotangent):
    half = shape(2, CUT, LANES)
    tokens = q_latent.shape[0]
    args = (q_latent, kv_latent, q_cotangent, kv_cotangent)
    scratch = [pltpu.VMEM(arg.shape, arg.dtype) for arg in args] + [pltpu.SemaphoreType.DMA((4,))]
    cost = pl.CostEstimate(flops=2 * tokens * 2 * 2 * CUT * LANES, bytes_accessed=8 << 20, transcendentals=0)
    a_send, b_send = call(send_kernel, (half, half), 4, scratch, pltpu.HBM, cost, 60)(*args)
    a_got = lax.ppermute(a_send, "x", PAIR)
    b_got = lax.ppermute(b_send, "zl", PAIR)
    a_keep, b_keep = call(keep_kernel, (half, half), 4, scratch, pltpu.HBM, cost, 24)(*args)
    a_next = lax.ppermute(a_keep[1] + a_got[1], "zl", PAIR)
    b_next = lax.ppermute(b_keep[1] + b_got[1], "x", PAIR)
    parts = (a_keep, a_got, a_next, b_keep, b_got, b_next)
    pieces = call(add_kernel, (shape(PIECE, LANES),) * PIECES, 6)(*parts)
    sums = lax.psum(tuple(pieces), "zh")
    leaving = jnp.concatenate(sums[: QMORE // PIECE], axis=0)
    other = lax.ppermute(leaving, "zl", [(1, 0)])
    rows = (pltpu.VMEM((QRANK, QDIM), F32), pltpu.VMEM((KVRANK, KVDIM), F32))
    ready = call(update_kernel, shape(4, QOWN, LANES), PIECES + 1, rows)(*sums, other)
    got = lax.all_to_all(ready, ("x", "zl"), 0, 0)
    return call(join_kernel, (shape(QOWN, 2 * QDIM), shape(KVOWN, 2 * KVDIM)), 1)(got)


def solution(mesh):
    fine = Mesh(mesh.devices.reshape(2, 8, 2, -1), ("x", "zh", "zl", "head"))
    rows = ("x", "zh", "zl")
    return jax.shard_map(
        body,
        mesh=fine,
        in_specs=(P(rows, None), P(rows, None), P(rows, "head"), P(rows, "head")),
        out_specs=(P(rows, "head"), P(rows, "head")),
        check_vma=False,
    )
```

```python
import math

import jax
import jax.numpy as jnp
from jax import lax
from jax.experimental import pallas as pl
from jax.experimental.pallas import tpu as pltpu
from jax.sharding import Mesh, PartitionSpec as P

QRANK = 1536
KVRANK = 512
QDIM = 192
KVDIM = 256
ITERS = 5
RESTART = 3

COEF_A = 3.4445
COEF_B = -4.775
COEF_C = 2.0315
EPSILON = 1e-06

LANES = 256
QTILES = QRANK // LANES
KVTILES = KVRANK // LANES
HEAD_ROWS = QTILES * QDIM + KVTILES * KVDIM
PART = HEAD_ROWS // 2
CUT = PART // 2
QHERE = PART // QDIM
QREST = PART - QHERE * QDIM
QMORE = QTILES * QDIM - PART
SIZES = (16,) * 38 + (8,) * 28
STARTS = tuple(sum(SIZES[:k]) for k in range(len(SIZES)))
PIECES = len(SIZES)
QOWN = QRANK // 32
KVOWN = KVRANK // 32
MEBI = 1024 * 1024
VMEM = pl.BlockSpec(memory_space=pltpu.VMEM)
F32 = jnp.float32


def dot(lhs, rhs, dims):
    return lax.dot_general(
        lhs, rhs, (dims, ((), ())), precision=lax.Precision.HIGHEST, preferred_element_type=F32
    )


def mul(lhs, rhs):
    return dot(lhs, rhs, ((1,), (0,)))


def products(cot, start, stop, lat):
    return lax.dot_general(
        cot[:, start:stop], lat, (((0,), (0,)), ((), ())), preferred_element_type=F32
    )


def fill(part, low, high, q_cot, kv_cot, ql, kl, out):
    base = part * PART
    at = base + low
    while at < base + high:
        in_q = at < QTILES * QDIM
        width, first, cot, lat = (QDIM, 0, q_cot, ql) if in_q else (KVDIM, QTILES * QDIM, kv_cot, kl)
        tile, start = divmod(at - first, width)
        stop = min(width, start + base + high - at)
        block = products(cot, start, stop, lat[:, tile * LANES : (tile + 1) * LANES])
        out[at - base - low : at - base - low + stop - start, :] = block
        at += stop - start


def heads(qc, kc, x, away):
    second = (x ^ away) == 1
    q_cot = jnp.where(second, qc[:, QDIM:], qc[:, :QDIM])
    return q_cot, jnp.where(second, kc[:, KVDIM:], kc[:, :KVDIM])


def send_kernel(ql, kl, qc, kc, a_send, b_send, ql_v, kl_v, qc_v, kc_v, sems):
    x, z = lax.axis_index("x"), lax.axis_index("zl")
    pairs = ((qc, qc_v), (ql, ql_v), (kc, kc_v), (kl, kl_v))
    copies = [pltpu.make_async_copy(src, dst, sems.at[k]) for k, (src, dst) in enumerate(pairs)]
    for copy in copies:
        copy.start()
    copies[0].wait()
    copies[1].wait()
    q_cot = jnp.where(x == 0, qc_v[:, QDIM:], qc_v[:, :QDIM])
    fill(0, 0, CUT, q_cot, None, ql_v, None, a_send.at[z])
    copies[2].wait()
    copies[3].wait()
    q_cot, kv_cot = heads(qc_v, kc_v, x, 1)
    fill(1, 0, CUT, q_cot, kv_cot, ql_v, kl_v, a_send.at[z ^ 1])
    for part in range(2):

        @pl.when(z != part)
        def _(part=part):
            for away in range(2):
                q_cot, kv_cot = heads(qc_v, kc_v, x, away)
                fill(part, CUT, PART, q_cot, kv_cot, ql_v, kl_v, b_send.at[away])


def keep_kernel(ql, kl, qc, kc, a_keep, b_keep, ql_v, kl_v, qc_v, kc_v, sems):
    x, z = lax.axis_index("x"), lax.axis_index("zl")
    pairs = ((qc, qc_v), (kc, kc_v), (ql, ql_v), (kl, kl_v))
    copies = [pltpu.make_async_copy(src, dst, sems.at[k]) for k, (src, dst) in enumerate(pairs)]
    for copy in copies:
        copy.start()
    for copy in copies:
        copy.wait()
    q_cot, kv_cot = heads(qc_v, kc_v, x, 0)
    for part in range(2):
        fill(part, 0, CUT, q_cot, kv_cot, ql_v, kl_v, a_keep.at[z ^ part])
    for part in range(2):

        @pl.when(z == part)
        def _(part=part):
            for away in range(2):
                q_cot, kv_cot = heads(qc_v, kc_v, x, away)
                fill(part, CUT, PART, q_cot, kv_cot, ql_v, kl_v, b_keep.at[away])


def add_kernel(a_keep, a_got, a_next, b_keep, b_got, b_next, *outs):
    for k, out in enumerate(outs):
        low = STARTS[k]
        keep, got, last = (a_keep, a_got, a_next) if low < CUT else (b_keep, b_got, b_next)
        rows = slice(low % CUT, low % CUT + SIZES[k])
        out[...] = keep[0, rows, :] + got[0, rows, :] + last[rows, :]


def identity(size):
    rows = lax.broadcasted_iota(jnp.int32, (size, size), 0)
    return rows == lax.broadcasted_iota(jnp.int32, (size, size), 1)


def steps(gram, count):
    product = None
    for index in range(count):
        poly = COEF_B * gram + COEF_C * mul(gram, gram)
        if product is None:
            product = jnp.where(identity(poly.shape[0]), COEF_A + poly, poly)
        else:
            product = COEF_A * product + mul(product, poly)
        if index + 1 < count:
            inner = COEF_A * gram + mul(gram, poly)
            gram = COEF_A * inner + mul(poly, inner)
    return product


def gram_of(wide):
    def term(lhs, rhs):
        return lax.dot_general(lhs, rhs, (((1,), (1,)), ((), ())), preferred_element_type=F32)

    high = wide.astype(jnp.bfloat16)
    rest = wide - high.astype(F32)
    mid = rest.astype(jnp.bfloat16)
    low = (rest - mid.astype(F32)).astype(jnp.bfloat16)
    cross = term(high, mid) + (term(high, low) + 0.5 * term(mid, mid))
    return term(high, high) + (cross + cross.T)


def orthogonalize(tiles, norm, rows):
    wide = jnp.concatenate(tiles, axis=1)
    gram = gram_of(wide)
    trace = jnp.sum(jnp.where(identity(gram.shape[0]), gram, 0.0))
    scale = lax.rsqrt(jnp.full((1, 1), trace + EPSILON, F32))
    product = steps(gram * scale * scale, RESTART)
    wide = mul(product * scale, wide)
    product = steps(gram_of(wide), ITERS - RESTART)
    rows[...] = dot(wide, product * norm, ((0,), (0,)))


def update_kernel(*refs):
    pieces, (other, out, q_rows, kv_rows) = refs[:PIECES], refs[PIECES:]

    def y(low, high):
        return jnp.concatenate([ref[...] for ref, at in zip(pieces, STARTS) if low <= at < high], axis=0)

    z, high = lax.axis_index("zl"), lax.axis_index("zh")

    @pl.when(z == 0)
    def _():
        tiles = [y(t * QDIM, (t + 1) * QDIM) for t in range(QHERE)]
        tiles.append(jnp.concatenate((y(QHERE * QDIM, PART), other[: QDIM - QREST, :]), axis=0))
        tiles += [other[t * QDIM - PART : (t + 1) * QDIM - PART, :] for t in range(QHERE + 1, QTILES)]
        orthogonalize(tiles, math.sqrt(QRANK), q_rows)
        for half in range(2):
            for k in range(2):
                start = pl.multiple_of(half * (QRANK // 2) + (2 * high + k) * QOWN, 8)
                out[2 * half + k, :, :QDIM] = q_rows[pl.ds(start, QOWN), :]
                out[2 * half + k, :, QDIM:] = jnp.zeros((QOWN, LANES - QDIM), F32)

    @pl.when(z == 1)
    def _():
        tiles = [y(QMORE + t * KVDIM, QMORE + (t + 1) * KVDIM) for t in range(KVTILES)]
        orthogonalize(tiles, math.sqrt(KVRANK), kv_rows)
        for half in range(2):
            for k in range(2):
                start = pl.multiple_of(half * (KVRANK // 2) + (2 * high + k) * KVOWN, 8)
                out[2 * half + k, :KVOWN, :] = kv_rows[pl.ds(start, KVOWN), :]
                out[2 * half + k, KVOWN:, :] = jnp.zeros((QOWN - KVOWN, LANES), F32)


def join_kernel(got, q_out, kv_out):
    for head in range(2):
        q_out[:, head * QDIM : (head + 1) * QDIM] = got[2 * head, :, :QDIM]
        kv_out[:, head * KVDIM : (head + 1) * KVDIM] = got[2 * head + 1, :KVOWN, :]


def shape(*dims):
    return jax.ShapeDtypeStruct(dims, F32)


def call(kernel, outs, inputs, scratch=(), space=pltpu.VMEM, cost=None, vmem=24):
    single = not isinstance(outs, tuple)
    return pl.pallas_call(
        kernel,
        out_shape=outs,
        in_specs=[pl.BlockSpec(memory_space=space)] * inputs,
        out_specs=VMEM if single else (VMEM,) * len(outs),
        scratch_shapes=list(scratch),
        compiler_params=pltpu.CompilerParams(vmem_limit_bytes=vmem * MEBI),
        cost_estimate=cost,
    )


PAIR = [(0, 1), (1, 0)]


def body(q_latent, kv_latent, q_cotangent, kv_cotangent):
    half = shape(2, CUT, LANES)
    tokens = q_latent.shape[0]
    args = (q_latent, kv_latent, q_cotangent, kv_cotangent)
    scratch = [pltpu.VMEM(arg.shape, arg.dtype) for arg in args] + [pltpu.SemaphoreType.DMA((4,))]
    cost = pl.CostEstimate(flops=2 * tokens * 2 * 2 * CUT * LANES, bytes_accessed=8 << 20, transcendentals=0)
    a_send, b_send = call(send_kernel, (half, half), 4, scratch, pltpu.HBM, cost, 60)(*args)
    a_got = lax.ppermute(a_send, "x", PAIR)
    b_got = lax.ppermute(b_send, "zl", PAIR)
    a_keep, b_keep = call(keep_kernel, (half, half), 4, scratch, pltpu.HBM, cost, 24)(*args)
    a_next = lax.ppermute(a_keep[1] + a_got[1], "zl", PAIR)
    b_next = lax.ppermute(b_keep[1] + b_got[1], "x", PAIR)
    parts = (a_keep, a_got, a_next, b_keep, b_got, b_next)
    pieces = call(add_kernel, tuple(shape(size, LANES) for size in SIZES), 6)(*parts)
    sums = lax.psum(tuple(pieces), "zh")
    leaving = jnp.concatenate(sums[: STARTS.index(QMORE)], axis=0)
    other = lax.ppermute(leaving, "zl", [(1, 0)])
    rows = (pltpu.VMEM((QRANK, QDIM), F32), pltpu.VMEM((KVRANK, KVDIM), F32))
    ready = call(update_kernel, shape(4, QOWN, LANES), PIECES + 1, rows)(*sums, other)
    got = lax.all_to_all(ready, ("x", "zl"), 0, 0)
    return call(join_kernel, (shape(QOWN, 2 * QDIM), shape(KVOWN, 2 * KVDIM)), 1)(got)


def solution(mesh):
    fine = Mesh(mesh.devices.reshape(2, 8, 2, -1), ("x", "zh", "zl", "head"))
    rows = ("x", "zh", "zl")
    return jax.shard_map(
        body,
        mesh=fine,
        in_specs=(P(rows, None), P(rows, None), P(rows, "head"), P(rows, "head")),
        out_specs=(P(rows, "head"), P(rows, "head")),
        check_vma=False,
    )
```

```python
import math

import jax
import jax.numpy as jnp
from jax import lax
from jax.experimental import pallas as pl
from jax.experimental.pallas import tpu as pltpu
from jax.sharding import Mesh, PartitionSpec as P

QRANK = 1536
KVRANK = 512
QDIM = 192
KVDIM = 256
ITERS = 5
RESTART = 3

COEF_A = 3.4445
COEF_B = -4.775
COEF_C = 2.0315
EPSILON = 1e-06

LANES = 256
QTILES = QRANK // LANES
KVTILES = KVRANK // LANES
HEAD_ROWS = QTILES * QDIM + KVTILES * KVDIM
PART = HEAD_ROWS // 2
CUT = PART // 2
QHERE = PART // QDIM
QREST = PART - QHERE * QDIM
QMORE = QTILES * QDIM - PART
SIZES = (16,) * 38 + (8,) * 28
STARTS = tuple(sum(SIZES[:k]) for k in range(len(SIZES)))
PIECES = len(SIZES)
QOWN = QRANK // 32
KVOWN = KVRANK // 32
QSPAN = 256
KVSPAN = 128
MEBI = 1024 * 1024
VMEM = pl.BlockSpec(memory_space=pltpu.VMEM)
F32 = jnp.float32


def dot(lhs, rhs, dims):
    return lax.dot_general(
        lhs, rhs, (dims, ((), ())), precision=lax.Precision.HIGHEST, preferred_element_type=F32
    )


def mul(lhs, rhs):
    return dot(lhs, rhs, ((1,), (0,)))


def products(cot, start, stop, lat):
    return lax.dot_general(
        cot[:, start:stop], lat, (((0,), (0,)), ((), ())), preferred_element_type=F32
    )


def fill(part, low, high, q_cot, kv_cot, ql, kl, out):
    base = part * PART
    at = base + low
    while at < base + high:
        in_q = at < QTILES * QDIM
        width, first, cot, lat = (QDIM, 0, q_cot, ql) if in_q else (KVDIM, QTILES * QDIM, kv_cot, kl)
        tile, start = divmod(at - first, width)
        stop = min(width, start + base + high - at)
        block = products(cot, start, stop, lat[:, tile * LANES : (tile + 1) * LANES])
        out[at - base - low : at - base - low + stop - start, :] = block
        at += stop - start


def heads(qc, kc, x, away):
    second = (x ^ away) == 1
    q_cot = jnp.where(second, qc[:, QDIM:], qc[:, :QDIM])
    return q_cot, jnp.where(second, kc[:, KVDIM:], kc[:, :KVDIM])


def send_kernel(ql, kl, qc, kc, a_send, b_send, ql_v, kl_v, qc_v, kc_v, sems):
    x, z = lax.axis_index("x"), lax.axis_index("zl")
    pairs = ((qc, qc_v), (ql, ql_v), (kc, kc_v), (kl, kl_v))
    copies = [pltpu.make_async_copy(src, dst, sems.at[k]) for k, (src, dst) in enumerate(pairs)]
    for copy in copies:
        copy.start()
    copies[0].wait()
    copies[1].wait()
    q_cot = jnp.where(x == 0, qc_v[:, QDIM:], qc_v[:, :QDIM])
    fill(0, 0, CUT, q_cot, None, ql_v, None, a_send.at[z])
    copies[2].wait()
    copies[3].wait()
    q_cot, kv_cot = heads(qc_v, kc_v, x, 1)
    fill(1, 0, CUT, q_cot, kv_cot, ql_v, kl_v, a_send.at[z ^ 1])
    for part in range(2):

        @pl.when(z != part)
        def _(part=part):
            for away in range(2):
                q_cot, kv_cot = heads(qc_v, kc_v, x, away)
                fill(part, CUT, PART, q_cot, kv_cot, ql_v, kl_v, b_send.at[away])


def keep_kernel(ql, kl, qc, kc, a_keep, b_keep, ql_v, kl_v, qc_v, kc_v, sems):
    x, z = lax.axis_index("x"), lax.axis_index("zl")
    pairs = ((qc, qc_v), (kc, kc_v), (ql, ql_v), (kl, kl_v))
    copies = [pltpu.make_async_copy(src, dst, sems.at[k]) for k, (src, dst) in enumerate(pairs)]
    for copy in copies:
        copy.start()
    for copy in copies:
        copy.wait()
    q_cot, kv_cot = heads(qc_v, kc_v, x, 0)
    for part in range(2):
        fill(part, 0, CUT, q_cot, kv_cot, ql_v, kl_v, a_keep.at[z ^ part])
    for part in range(2):

        @pl.when(z == part)
        def _(part=part):
            for away in range(2):
                q_cot, kv_cot = heads(qc_v, kc_v, x, away)
                fill(part, CUT, PART, q_cot, kv_cot, ql_v, kl_v, b_keep.at[away])


def add_kernel(a_keep, a_got, a_next, b_keep, b_got, b_next, *outs):
    for k, out in enumerate(outs):
        low = STARTS[k]
        keep, got, last = (a_keep, a_got, a_next) if low < CUT else (b_keep, b_got, b_next)
        rows = slice(low % CUT, low % CUT + SIZES[k])
        out[...] = keep[0, rows, :] + got[0, rows, :] + last[rows, :]


def identity(size):
    rows = lax.broadcasted_iota(jnp.int32, (size, size), 0)
    return rows == lax.broadcasted_iota(jnp.int32, (size, size), 1)


def steps(gram, count):
    product = None
    for index in range(count):
        poly = COEF_B * gram + COEF_C * mul(gram, gram)
        if product is None:
            product = jnp.where(identity(poly.shape[0]), COEF_A + poly, poly)
        else:
            product = COEF_A * product + mul(product, poly)
        if index + 1 < count:
            inner = COEF_A * gram + mul(gram, poly)
            gram = COEF_A * inner + mul(poly, inner)
    return product


def gram_of(wide):
    def term(lhs, rhs):
        return lax.dot_general(lhs, rhs, (((1,), (1,)), ((), ())), preferred_element_type=F32)

    high = wide.astype(jnp.bfloat16)
    rest = wide - high.astype(F32)
    mid = rest.astype(jnp.bfloat16)
    low = (rest - mid.astype(F32)).astype(jnp.bfloat16)
    cross = term(high, mid) + (term(high, low) + 0.5 * term(mid, mid))
    return term(high, high) + (cross + cross.T)


def orthogonalize(tiles, norm, own, span, wide_v, rows):
    wide = jnp.concatenate(tiles, axis=1)
    gram = gram_of(wide)
    trace = jnp.sum(jnp.where(identity(gram.shape[0]), gram, 0.0))
    scale = lax.rsqrt(jnp.full((1, 1), trace + EPSILON, F32))
    product = steps(gram * scale * scale, RESTART)
    wide = mul(product * scale, wide)
    product = steps(gram_of(wide), ITERS - RESTART)
    wide_v[...] = wide
    half_lanes = wide.shape[1] // 2
    first = jnp.minimum((own // 128) * 128, half_lanes - span)
    for half in range(2):
        lanes = pl.ds(pl.multiple_of(half * half_lanes + first, 128), span)
        rows[half] = dot(wide_v[:, lanes], product * norm, ((0,), (0,)))
    return own - first


def update_kernel(*refs):
    pieces, (other, out, q_wide, kv_wide, q_rows, kv_rows) = refs[:PIECES], refs[PIECES:]

    def y(low, high):
        return jnp.concatenate([ref[...] for ref, at in zip(pieces, STARTS) if low <= at < high], axis=0)

    z, high = lax.axis_index("zl"), lax.axis_index("zh")

    @pl.when(z == 0)
    def _():
        tiles = [y(t * QDIM, (t + 1) * QDIM) for t in range(QHERE)]
        tiles.append(jnp.concatenate((y(QHERE * QDIM, PART), other[: QDIM - QREST, :]), axis=0))
        tiles += [other[t * QDIM - PART : (t + 1) * QDIM - PART, :] for t in range(QHERE + 1, QTILES)]
        at = orthogonalize(tiles, math.sqrt(QRANK), high * (2 * QOWN), QSPAN, q_wide, q_rows)
        for half in range(2):
            for k in range(2):
                start = pl.multiple_of(at + k * QOWN, 8)
                out[2 * half + k, :, :QDIM] = q_rows[half, pl.ds(start, QOWN), :]
                out[2 * half + k, :, QDIM:] = jnp.zeros((QOWN, LANES - QDIM), F32)

    @pl.when(z == 1)
    def _():
        tiles = [y(QMORE + t * KVDIM, QMORE + (t + 1) * KVDIM) for t in range(KVTILES)]
        at = orthogonalize(tiles, math.sqrt(KVRANK), high * (2 * KVOWN), KVSPAN, kv_wide, kv_rows)
        for half in range(2):
            for k in range(2):
                start = pl.multiple_of(at + k * KVOWN, 8)
                out[2 * half + k, :KVOWN, :] = kv_rows[half, pl.ds(start, KVOWN), :]
                out[2 * half + k, KVOWN:, :] = jnp.zeros((QOWN - KVOWN, LANES), F32)


def join_kernel(got, q_out, kv_out):
    for head in range(2):
        q_out[:, head * QDIM : (head + 1) * QDIM] = got[2 * head, :, :QDIM]
        kv_out[:, head * KVDIM : (head + 1) * KVDIM] = got[2 * head + 1, :KVOWN, :]


def shape(*dims):
    return jax.ShapeDtypeStruct(dims, F32)


def call(kernel, outs, inputs, scratch=(), space=pltpu.VMEM, cost=None, vmem=24):
    single = not isinstance(outs, tuple)
    return pl.pallas_call(
        kernel,
        out_shape=outs,
        in_specs=[pl.BlockSpec(memory_space=space)] * inputs,
        out_specs=VMEM if single else (VMEM,) * len(outs),
        scratch_shapes=list(scratch),
        compiler_params=pltpu.CompilerParams(vmem_limit_bytes=vmem * MEBI),
        cost_estimate=cost,
    )


PAIR = [(0, 1), (1, 0)]


def body(q_latent, kv_latent, q_cotangent, kv_cotangent):
    half = shape(2, CUT, LANES)
    tokens = q_latent.shape[0]
    args = (q_latent, kv_latent, q_cotangent, kv_cotangent)
    scratch = [pltpu.VMEM(arg.shape, arg.dtype) for arg in args] + [pltpu.SemaphoreType.DMA((4,))]
    cost = pl.CostEstimate(flops=2 * tokens * 2 * 2 * CUT * LANES, bytes_accessed=8 << 20, transcendentals=0)
    a_send, b_send = call(send_kernel, (half, half), 4, scratch, pltpu.HBM, cost, 60)(*args)
    a_got = lax.ppermute(a_send, "x", PAIR)
    b_got = lax.ppermute(b_send, "zl", PAIR)
    a_keep, b_keep = call(keep_kernel, (half, half), 4, scratch, pltpu.HBM, cost, 24)(*args)
    a_next = lax.ppermute(a_keep[1] + a_got[1], "zl", PAIR)
    b_next = lax.ppermute(b_keep[1] + b_got[1], "x", PAIR)
    parts = (a_keep, a_got, a_next, b_keep, b_got, b_next)
    pieces = call(add_kernel, tuple(shape(size, LANES) for size in SIZES), 6)(*parts)
    sums = lax.psum(tuple(pieces), "zh")
    leaving = jnp.concatenate(sums[: STARTS.index(QMORE)], axis=0)
    other = lax.ppermute(leaving, "zl", [(1, 0)])
    rows = [
        pltpu.VMEM(dims, F32)
        for dims in ((QDIM, QRANK), (KVDIM, KVRANK), (2, QSPAN, QDIM), (2, KVSPAN, KVDIM))
    ]
    ready = call(update_kernel, shape(4, QOWN, LANES), PIECES + 1, rows)(*sums, other)
    got = lax.all_to_all(ready, ("x", "zl"), 0, 0)
    return call(join_kernel, (shape(QOWN, 2 * QDIM), shape(KVOWN, 2 * KVDIM)), 1)(got)


def solution(mesh):
    fine = Mesh(mesh.devices.reshape(2, 8, 2, -1), ("x", "zh", "zl", "head"))
    rows = ("x", "zh", "zl")
    return jax.shard_map(
        body,
        mesh=fine,
        in_specs=(P(rows, None), P(rows, None), P(rows, "head"), P(rows, "head")),
        out_specs=(P(rows, "head"), P(rows, "head")),
        check_vma=False,
    )
```
